32 devices in a mesh: group: 2 (over x), tile: 16 (over z, y, core).
Axes of the slice: x: 2, y: 2, z: 4, core: 2. Of those that a mesh axis runs over, the one named last changes fastest.
Arguments:
- wave_phase: float32 [600, 256], replicated, may hold values from -3.140625 to 3.140625
- tile_at: int32 [8, 16], replicated, may hold values from 0 to 127, as said below
- aperture_block: int32 [8], P('group'), parts along dimension 0, may hold values from 0 to 1
- source_cell: int32 [8, 2], P('group'), parts along dimension 0, may hold values from 0 to 255
- freq_index: int32 [8, 2], P('group'), parts along dimension 0, may hold values from 0 to 599
- observed: float32 [32, 2, 2, 64, 256], P(('group', 'tile')), parts along dimension 0, may hold values from -6 to 6
- image: float32 [256, 4, 1024], P(('group', 'tile')), parts along dimension 0, may hold values from -3 to 3
- slowness: float32 [256, 4, 1024], P(('group', 'tile')), parts along dimension 0, may hold values from -1 to 1
Outputs:
- gradient: float32 [256, 4, 1024], P(('group', 'tile')), parts along dimension 0
The draws below stay inside these ranges and needn't reach their ends.
There are 2 independent parts, one for each index of `group`. The reference program is written for one: setup_inputs(seed, part) draws one part's arguments, and reference() takes and returns one part's arrays. A program takes and returns all parts, laid end to end along the dimension named above; an argument that names none is the same for every part. Nothing has to cross between parts.
Inputs may be any that keep to these rules, and one draw needn't show every extreme that they name: `tile_at`: A permutation of the 128 tile numbers; in every window (tile columns b * 8 to b * 8 + 7) each value of t // 8 that occurs there occurs for exactly 4 tiles.
All inputs are finite; a program needn't handle non-finite values.
Results may differ from the reference program's by a relative error of at most 0.0003.
Values sent between devices are 32-bit elements; how exact they have to be, the bound alone decides.
A program may use at most 64 MiB of HBM per device.

```python
import math
import jax
import jax.numpy as jnp
import numpy as np
from jax import lax

A = 256
TL = 32
SECTIONS = 4
LEV = 1
NF = 2
NFT = 600
TILES_DEV = 8
SLOTS = 4
NZ = 4
SIDE = 8
NT = 128
NB = 2
ROWS = 64
N_TILE = 16


def draw_tile_at(key, part):
    per_window = SIDE * SIDE
    mixed = jax.random.fold_in(key, 7)
    round_keys = jax.random.split(jax.random.fold_in(mixed, 1), TILES_DEV)
    owner_rounds = jax.vmap(lambda round_key: jax.random.permutation(round_key, N_TILE))(round_keys)
    block_keys = jax.random.split(jax.random.fold_in(mixed, 2), NB)
    local_order = jax.vmap(lambda block_key: jax.random.permutation(block_key, per_window))(block_keys)
    flat_slot = jnp.arange(NB, dtype=jnp.int32)[:, None] * per_window + local_order.astype(jnp.int32)
    round_index = flat_slot // N_TILE
    owner_device = owner_rounds[round_index, flat_slot % N_TILE].astype(jnp.int32)
    tile_number = owner_device * TILES_DEV + round_index
    return tile_number.reshape(NB, SIDE, SIDE).transpose(1, 0, 2).reshape(SIDE, NB * SIDE).astype(jnp.int32)


def set_ends(values, rng, smallest, high):
    shape = values.shape
    place = [jax.random.randint(jax.random.fold_in(rng, axis), (), 0, shape[axis]) for axis in range(len(shape))]
    values = values.at[tuple(place)].set(smallest)
    longest = shape.index(max(shape))
    place[longest] = (place[longest] + 1) % shape[longest]
    return values.at[tuple(place)].set(high)


def levels(key, extent, cuts, low, top_value):
    level = 1.0
    for dim, parts in cuts:
        steps = jax.random.uniform(jax.random.fold_in(jax.random.fold_in(key, 6), dim), (parts,), jnp.float32, low / len(cuts), top_value / len(cuts))
        level = level * jnp.repeat(jnp.exp(steps), extent[dim] // parts).reshape((-1,) + (1,) * (len(extent) - 1 - dim))
    return level


def rank_table(amount, lean):
    loads = [(1 << 20) // math.isqrt(grade ** lean) + 1 for grade in range(1, amount + 1)]
    spread = 1 + sum(loads) // (1 << 30)
    return np.cumsum(np.array([max(1, weight // spread) for weight in loads]))


def ranked_ids(rng, shape, count, lean):
    table = rank_table(count, lean)
    lot = jax.random.randint(jax.random.fold_in(rng, 1), shape, 0, int(table[count - 1]))
    grade = jnp.searchsorted(jnp.asarray(table, jnp.int32), lot, side="right")
    return jax.random.permutation(jax.random.fold_in(rng, 2), count)[grade].astype(jnp.int32)


def centred(stream_key, extent, spread, limit, cuts=(), kind=jnp.bfloat16):
    result = jax.random.normal(stream_key, extent, jnp.float32) * spread
    if len(cuts) > 0:
        result = levels(stream_key, extent, cuts, -0.22, 0.18) * result
    return jnp.clip(result, min=-limit, max=limit).astype(kind)


def setup_inputs(seed: int = 0, part: int = 0) -> dict:
    keys = jax.random.split(jax.random.key(seed), 9)
    part_keys = jax.random.split(jax.random.fold_in(keys[8], part), 9)
    wave_phase = jnp.clip(jax.random.uniform(keys[0], (NFT, A), jnp.float32, -3.140625, 3.140625), -3.140625, 3.140625)
    tile_at = draw_tile_at(jax.random.fold_in(keys[8], 71), part)
    aperture_block = set_ends(ranked_ids(part_keys[2], (SLOTS,), NB, 2), jax.random.fold_in(part_keys[2], 3), 0, NB - 1).astype(jnp.int32)
    source_cell = set_ends(jax.random.randint(part_keys[3], (SLOTS, 2), 0, A), jax.random.fold_in(part_keys[3], 1), 0, A - 1).astype(jnp.int32)
    freq_index = set_ends(jax.random.randint(part_keys[4], (SLOTS, NF), 0, NFT), jax.random.fold_in(part_keys[4], 1), 0, NFT - 1).astype(jnp.int32)
    observed = centred(part_keys[5], (N_TILE, NF, 2, ROWS, A), 1.0, 6.0, ((0, 16),), jnp.float32)
    image = centred(part_keys[6], (NT, NZ, TL * TL), 0.5, 3.0, ((0, 16),), jnp.float32)
    slowness = jnp.clip(jax.random.uniform(part_keys[7], (NT, NZ, TL * TL), jnp.float32, -1.0, 1.0) * levels(part_keys[7], (NT, NZ, TL * TL), ((0, 16),), -0.4, 0.0), -1.0, 1.0)
    return {"wave_phase": wave_phase, "tile_at": tile_at, "aperture_block": aperture_block, "source_cell": source_cell, "freq_index": freq_index, "observed": observed, "image": image, "slowness": slowness}


LENS_GAIN = 3.0
FINEST = lax.Precision.HIGHEST


def circulant(coef):
    length = coef.shape[1]
    shifted = jnp.concatenate([coef[:, 1:], coef[:, :1]], axis=1)
    tiled = jnp.tile(shifted, (1, length + 1))
    return tiled.reshape(coef.shape[0], length, length + 1)[:, :, :length][:, :, ::-1]


def build_operator(wave_phase, chosen_freqs):
    length = wave_phase.shape[1]
    phase_rows = wave_phase[chosen_freqs]
    spin_index = jnp.arange(length, dtype=jnp.int32)
    turn_table = (spin_index[:, None] * spin_index[None, :]) % length
    angles = phase_rows[:, :, None] + (2.0 * math.pi / length) * turn_table[None, :, :].astype(jnp.float32)
    coef_real = jnp.mean(jnp.cos(angles), axis=1)
    coef_imag = jnp.mean(jnp.sin(angles), axis=1)
    return jnp.stack([circulant(coef_real), circulant(coef_imag)], axis=1)


def left_product(operator, values):
    real_part = (jnp.einsum("fij,fjk->fik", operator[:, 0], values[:, 0], precision=FINEST)
                 - jnp.einsum("fij,fjk->fik", operator[:, 1], values[:, 1], precision=FINEST))
    imag_part = (jnp.einsum("fij,fjk->fik", operator[:, 0], values[:, 1], precision=FINEST)
                 + jnp.einsum("fij,fjk->fik", operator[:, 1], values[:, 0], precision=FINEST))
    return jnp.stack([real_part, imag_part], axis=1)


def right_transpose(values, operator):
    real_part = (jnp.einsum("fij,fkj->fik", values[:, 0], operator[:, 0], precision=FINEST)
                 - jnp.einsum("fij,fkj->fik", values[:, 1], operator[:, 1], precision=FINEST))
    imag_part = (jnp.einsum("fij,fkj->fik", values[:, 0], operator[:, 1], precision=FINEST)
                 + jnp.einsum("fij,fkj->fik", values[:, 1], operator[:, 0], precision=FINEST))
    return jnp.stack([real_part, imag_part], axis=1)


def left_adjoint(operator, values):
    real_part = (jnp.einsum("fji,fjk->fik", operator[:, 0], values[:, 0], precision=FINEST)
                 + jnp.einsum("fji,fjk->fik", operator[:, 1], values[:, 1], precision=FINEST))
    imag_part = (jnp.einsum("fji,fjk->fik", operator[:, 0], values[:, 1], precision=FINEST)
                 - jnp.einsum("fji,fjk->fik", operator[:, 1], values[:, 0], precision=FINEST))
    return jnp.stack([real_part, imag_part], axis=1)


def right_conjugate(values, operator):
    real_part = (jnp.einsum("fij,fjk->fik", values[:, 0], operator[:, 0], precision=FINEST)
                 + jnp.einsum("fij,fjk->fik", values[:, 1], operator[:, 1], precision=FINEST))
    imag_part = (jnp.einsum("fij,fjk->fik", values[:, 1], operator[:, 0], precision=FINEST)
                 - jnp.einsum("fij,fjk->fik", values[:, 0], operator[:, 1], precision=FINEST))
    return jnp.stack([real_part, imag_part], axis=1)


def complex_times(factor, values):
    real_part = factor[:, 0] * values[:, 0] - factor[:, 1] * values[:, 1]
    imag_part = factor[:, 0] * values[:, 1] + factor[:, 1] * values[:, 0]
    return jnp.stack([real_part, imag_part], axis=1)


def conjugate_times(factor, values):
    real_part = factor[:, 0] * values[:, 0] + factor[:, 1] * values[:, 1]
    imag_part = factor[:, 0] * values[:, 1] - factor[:, 1] * values[:, 0]
    return jnp.stack([real_part, imag_part], axis=1)


def extend(operator, lens_part, values):
    return right_transpose(left_product(operator, complex_times(lens_part, values)), operator)


def retract(operator, lens_part, values, offset):
    product = left_adjoint(operator, values)
    if offset is not None:
        product = product - offset
    return conjugate_times(lens_part, right_conjugate(product, operator))


def born_term(angular, reflect, source_part):
    weights = angular[:, None, None] * reflect[None, :, :]
    return jnp.stack([-weights * source_part[:, 1], weights * source_part[:, 0]], axis=1)


def imaging_term(angular, adjoint_part, source_part):
    return jnp.sum(angular[:, None, None] * (adjoint_part[:, 1] * source_part[:, 0] - adjoint_part[:, 0] * source_part[:, 1]), axis=0)


def reference(wave_phase, tile_at, aperture_block, source_cell, freq_index, observed, image, slowness):
    window_side = A // TL
    column_count = N_TILE // SECTIONS
    depth_total = SECTIONS * LEV
    cell_count = TL * TL
    per_window = window_side * window_side
    observed_rows = observed.reshape(SECTIONS, column_count, NF, 2, A // SECTIONS, A)
    cell_index = jnp.arange(A, dtype=jnp.int32)

    def one_shot(totals, my_column):
        block_id = aperture_block[my_column]
        window_ids = lax.dynamic_slice(tile_at, (jnp.int32(0), (block_id * window_side).astype(jnp.int32)), (window_side, window_side)).reshape(per_window)

        def to_window(tiled):
            return tiled[window_ids].reshape(window_side, window_side, depth_total, TL, TL).transpose(2, 0, 3, 1, 4).reshape(depth_total, A, A)

        reflect = to_window(image)
        chosen_freqs = freq_index[my_column]
        angular = (chosen_freqs + 1).astype(jnp.float32) / NFT
        operator = build_operator(wave_phase, chosen_freqs)
        angles = LENS_GAIN * angular[None, :, None, None] * to_window(slowness)[:, None, :, :]
        lens_table = jnp.stack([jnp.cos(angles), jnp.sin(angles)], axis=2)
        recorded = jnp.transpose(observed_rows[:, my_column], (1, 2, 0, 3, 4)).reshape(NF, 2, A, A)
        spike_field = ((cell_index[:, None] == source_cell[my_column, 0]) & (cell_index[None, :] == source_cell[my_column, 1])).astype(jnp.float32) * A
        source = jnp.stack([jnp.broadcast_to(spike_field, (NF, A, A)), jnp.zeros((NF, A, A), jnp.float32)], axis=1)

        def down_step(values, lens_part):
            values = extend(operator, lens_part, values)
            return values, values

        last_source, source_levels = lax.scan(down_step, source, lens_table)

        def up_step(values, inputs):
            lens_part, reflect_part, source_part = inputs
            return extend(operator, lens_part, values + born_term(angular, reflect_part, source_part)), None

        surface, unused = lax.scan(up_step, jnp.zeros_like(source), (lens_table, reflect, source_levels), reverse=True)

        def back_step(values, inputs):
            lens_part, source_part = inputs
            values = retract(operator, lens_part, values, None)
            return values, imaging_term(angular, values, source_part)

        last_back, images = lax.scan(back_step, surface - recorded, (lens_table, source_levels))
        tiles_out = images.reshape(depth_total, window_side, TL, window_side, TL).transpose(1, 3, 0, 2, 4).reshape(per_window, depth_total, cell_count)
        return totals.at[window_ids].add(tiles_out), None

    totals, unused = lax.scan(one_shot, jnp.zeros(image.shape, jnp.float32), jnp.arange(column_count, dtype=jnp.int32))
    return totals
```

```python
import functools
import math

import jax
import jax.numpy as jnp
import numpy as np
from jax import lax
from jax.experimental import pallas as pl
from jax.experimental.pallas import tpu as pltpu
from jax.sharding import PartitionSpec as P

A = 256
TL = 32
SIDE = A // TL
CELLS = SIDE * SIDE
SECTIONS = 4
NZ = 4
NF = 2
NFT = 600
ROWS = A // SECTIONS
LENS_GAIN = 3.0
VMEM_LIMIT = 56 * 1024 * 1024

F32 = jnp.float32
BF16 = jnp.bfloat16


def sin_cos(angle):
    t = angle * 0.5
    u = t * t
    s = -1.0 / math.factorial(11)
    for n in (9, 7, 5, 3, 1):
        s = s * u + (-1.0) ** (n // 2) / math.factorial(n)
    s = s * t
    c = 1.0 / math.factorial(12)
    for n in (10, 8, 6, 4, 2, 0):
        c = c * u + (-1.0) ** (n // 2) / math.factorial(n)
    return 2.0 * s * c, 1.0 - 2.0 * s * s


def split(values):
    high = values.astype(BF16)
    return high, (values - high.astype(F32)).astype(BF16)


def dot(a, b):
    return lax.dot_general(a, b, (((1,), (0,)), ((), ())), preferred_element_type=F32)


def split_dot_left(op_high, op_low, values):
    high, low = split(values)
    return dot(op_high, high) + dot(op_high, low) + dot(op_low, high)


def split_dot_right(values, op_high, op_low):
    high, low = split(values)
    return dot(high, op_high) + dot(high, op_low) + dot(low, op_high)


def swap_groups(tiles):
    lane = lax.broadcasted_iota(jnp.int32, tiles[0].shape, tiles[0].ndim - 1)
    axis = tiles[0].ndim - 1

    def exchange(low, high, width, first):
        return (
            jnp.where(first, low, pltpu.roll(high, width, axis)),
            jnp.where(first, pltpu.roll(low, 128 - width, axis), high),
        )

    first = lane < 64
    a0, a2 = exchange(tiles[0], tiles[2], 64, first)
    a1, a3 = exchange(tiles[1], tiles[3], 64, first)
    first = (lane & 32) == 0
    b0, b1 = exchange(a0, a1, 32, first)
    b2, b3 = exchange(a2, a3, 32, first)
    return b0, b1, b2, b3


def greet_all(me, count):
    barrier = pltpu.get_barrier_semaphore()

    def signal(step, carry):
        pl.semaphore_signal(
            barrier,
            inc=1,
            device_id={"tile": lax.rem(me + step, count)},
            device_id_type=pl.DeviceIdType.MESH,
        )
        return carry

    lax.fori_loop(1, count, signal, 0)
    pl.semaphore_wait(barrier, count - 1)


def remote(src, dst, send_sem, recv_sem, target):
    return pltpu.make_async_remote_copy(
        src_ref=src,
        dst_ref=dst,
        send_sem=send_sem,
        recv_sem=recv_sem,
        device_id={"tile": target},
        device_id_type=pl.DeviceIdType.MESH,
    )


def scatter_kernel(
    count, cap, picks, model, observed, got_model, got_rows, packed, send_sem, recv_sem, row_send, row_recv, local_sem
):
    me = lax.axis_index("tile")
    shots = count // SECTIONS
    pairs = shots * NF
    pair = me // 2
    computes = lax.rem(me, 2) == 0
    section, column = me // shots, lax.rem(me, shots)
    greet_all(me, count)

    def rows_copy(freq):
        return remote(
            observed.at[freq], got_rows.at[section], row_send.at[freq], row_recv.at[section], 2 * (NF * column + freq)
        )

    for freq in range(NF):
        there = 2 * (NF * column + freq)

        @pl.when(there != me)
        def _():
            rows_copy(freq).start()

        @pl.when(there == me)
        def _():
            keep = pltpu.make_async_copy(observed.at[freq], got_rows.at[section], local_sem)
            keep.start()
            keep.wait()

    def pack(slot, carry):
        packed[slot] = model[picks[slot]]
        return carry

    lax.fori_loop(0, shots * cap, pack, 0)

    def model_copy(to):
        return remote(
            packed.at[pl.ds((to // NF) * cap, cap)],
            got_model.at[pl.ds(me * cap, cap)],
            send_sem.at[to],
            recv_sem.at[me],
            2 * to,
        )

    def send(step, carry):
        to = lax.rem(pair + step, pairs)

        @pl.when(2 * to != me)
        def _():
            model_copy(to).start()

        @pl.when(2 * to == me)
        def _():
            keep = pltpu.make_async_copy(
                packed.at[pl.ds((to // NF) * cap, cap)], got_model.at[pl.ds(me * cap, cap)], local_sem
            )
            keep.start()
            keep.wait()

        return carry

    lax.fori_loop(0, pairs, send, 0)

    @pl.when(computes)
    def _():
        def arrive(step, carry):
            source = lax.rem(me + step, count)
            remote(
                packed.at[pl.ds(0, cap)], got_model.at[pl.ds(source * cap, cap)], send_sem.at[0], recv_sem.at[source], source
            ).wait_recv()
            return carry

        lax.fori_loop(1, count, arrive, 0)
        for part in range(SECTIONS):

            @pl.when(part * shots + pair // NF != me)
            def _():
                remote(observed.at[0], got_rows.at[part], row_send.at[0], row_recv.at[part], me + 1).wait_recv()

    def sent(to, carry):
        @pl.when(2 * to != me)
        def _():
            model_copy(to).wait_send()

        return carry

    lax.fori_loop(0, pairs, sent, 0)
    for freq in range(NF):

        @pl.when(2 * (NF * column + freq) != me)
        def _():
            rows_copy(freq).wait_send()


def march_kernel(
    numbers,
    window_slot,
    angular_ref,
    phase,
    table_cos,
    table_sin,
    model,
    rows,
    tiles_out,
    slow,
    reflect,
    lens,
    fields,
    spare,
    left_ops,
    right_ops,
):
    @pl.when(numbers[0] == 1)
    def _():
        angular = angular_ref[0]
        s, c = sin_cos(jnp.broadcast_to(phase[...], (8, A)))

        def table_dot(a, b):
            return lax.dot_general(
                a, b, (((1,), (0,)), ((), ())), preferred_element_type=F32, precision=lax.Precision.HIGHEST
            )

        c_cos, c_sin = table_dot(c, table_cos[...]), table_dot(c, table_sin[...])
        s_cos, s_sin = table_dot(s, table_cos[...]), table_dot(s, table_sin[...])
        scale = 1.0 / A

        def turned(row):
            return pltpu.roll(jnp.broadcast_to(row[0:1], (A, A)), 0, 1, stride=1, stride_axis=0)

        o_re, o_im = turned((c_cos + s_sin) * scale), turned((s_cos - c_sin) * scale)
        t_re, t_im = turned((c_cos - s_sin) * scale), turned((s_cos + c_sin) * scale)

        def put(ref, which, blocks):
            for i, block in enumerate(blocks):
                high, low = split(block)
                at = (pl.ds((i // 2) * A, A), pl.ds((i % 2) * A, A))
                ref[(2 * which, *at)] = high
                ref[(2 * which + 1, *at)] = low

        put(left_ops, 0, (o_re, -o_im, o_im, o_re))
        put(left_ops, 1, (t_re, t_im, -t_im, t_re))
        put(right_ops, 0, (t_re, t_im, -t_im, t_re))
        put(right_ops, 1, (o_re, -o_im, o_im, o_re))

        def gather(block_row, carry):
            for half in range(SIDE // 4):
                tiles = [model[window_slot[block_row * SIDE + half * 4 + j]] for j in range(4)]
                for k, part in enumerate(swap_groups(tiles)):
                    at = (half, pl.ds(block_row * TL + k, 8, stride=4))
                    for z in range(NZ):
                        reflect[(z, *at)] = part[z]
                        slow[(z, *at)] = part[NZ + z]
            return carry

        lax.fori_loop(0, SIDE, gather, 0)

        def whole(ref, z):
            return jnp.concatenate([ref[z, 0], ref[z, 1]], axis=1)

        def make_lens(z, carry):
            s, c = sin_cos(whole(slow, z) * (LENS_GAIN * angular))
            lens[z, 0] = c
            lens[z, 1] = s
            return carry

        lax.fori_loop(0, NZ, make_lens, 0)

        def extend(z, re, im):
            c, s = lens[z, 0], lens[z, 1]
            stacked = jnp.concatenate([c * re - s * im, c * im + s * re], axis=0)
            left = split_dot_left(left_ops[0], left_ops[1], stacked)
            beside = jnp.concatenate([left[:A], left[A:]], axis=1)
            right = split_dot_right(beside, right_ops[0], right_ops[1])
            return right[:, :A], right[:, A:]

        row_id = lax.broadcasted_iota(jnp.int32, (A, A), 0)
        column_id = lax.broadcasted_iota(jnp.int32, (A, A), 1)
        spike = jnp.where((row_id == numbers[1]) & (column_id == numbers[2]), float(A), 0.0).astype(F32)
        spare[0] = spike
        spare[1] = jnp.zeros((A, A), F32)

        def down(z, carry):
            re, im = extend(z, spare[0], spare[1])
            spare[0] = re
            spare[1] = im
            fields[z, 0] = re
            fields[z, 1] = im
            return carry

        lax.fori_loop(0, NZ, down, 0)
        spare[...] = jnp.zeros_like(spare)

        def up(step, carry):
            z = NZ - 1 - step
            weight = whole(reflect, z) * angular
            re, im = extend(z, spare[0] - weight * fields[z, 1], spare[1] + weight * fields[z, 0])
            spare[0] = re
            spare[1] = im
            return carry

        lax.fori_loop(0, NZ, up, 0)
        for part in range(SECTIONS):
            for half in range(2):
                at = (half, pl.ds(part * ROWS, ROWS))
                spare[at] = spare[at] - rows[part, half]

        def back(z, carry):
            left = split_dot_left(left_ops[2], left_ops[3], jnp.concatenate([spare[0], spare[1]], axis=0))
            beside = jnp.concatenate([left[:A], left[A:]], axis=1)
            right = split_dot_right(beside, right_ops[2], right_ops[3])
            re, im = right[:, :A], right[:, A:]
            c, s = lens[z, 0], lens[z, 1]
            re, im = c * re + s * im, c * im - s * re
            spare[0] = re
            spare[1] = im
            partial = angular * (im * fields[z, 0] - re * fields[z, 1])
            slow[z, 0] = partial[:, :128]
            slow[z, 1] = partial[:, 128:]
            return carry

        lax.fori_loop(0, NZ, back, 0)

        def give(block_row, carry):
            for half in range(SIDE // 4):
                parts = []
                for k in range(4):
                    at = (half, pl.ds(block_row * TL + k, 8, stride=4))
                    parts.append(jnp.stack([slow[(z, *at)] for z in range(NZ)]))
                for j, tile in enumerate(swap_groups(parts)):
                    tiles_out[block_row * SIDE + half * 4 + j] = tile
            return carry

        lax.fori_loop(0, SIDE, give, 0)


def return_kernel(
    count, cap, places, owned, ranks, homes, blocks, tiles, out, got, packed, send_sem, recv_sem, local_sem
):
    me = lax.axis_index("tile")
    shots = count // SECTIONS
    pairs = shots * NF
    pair = me // 2
    computes = lax.rem(me, 2) == 0
    greet_all(me, count)

    def tile_copy(to):
        return remote(packed.at[to], got.at[pair], send_sem.at[to], recv_sem.at[pair], to)

    @pl.when(computes)
    def _():
        def send(step, carry):
            to = lax.rem(me + step, count)
            for slot in range(cap):
                packed[to, slot] = tiles[places[to * cap + slot]]

            @pl.when(to != me)
            def _():
                tile_copy(to).start()

            @pl.when(to == me)
            def _():
                keep = pltpu.make_async_copy(packed.at[to], got.at[pair], local_sem)
                keep.start()
                keep.wait()

            return carry

        lax.fori_loop(0, count, send, 0)

    def arrive(source, carry):
        @pl.when(2 * source != me)
        def _():
            remote(packed.at[0], got.at[source], send_sem.at[0], recv_sem.at[source], 2 * source).wait_recv()

        return carry

    lax.fori_loop(0, pairs, arrive, 0)
    for tile in range(owned):

        def add(source, total):
            mine = homes[tile] == blocks[source // NF]
            return total + jnp.where(mine, got[source, ranks[tile]], 0.0)

        out[tile] = lax.fori_loop(0, pairs, add, jnp.zeros((NZ, 8, 128), F32))

    @pl.when(computes)
    def _():
        def sent(step, carry):
            tile_copy(lax.rem(me + step, count)).wait_send()
            return carry

        lax.fori_loop(1, count, sent, 0)


def total_of(values, axis):
    return jnp.sum(values, axis=axis, dtype=jnp.int32)


def shards(wave_phase, tile_at, aperture_block, source_cell, freq_index, observed, image, slowness):
    count = lax.axis_size("tile")
    me = lax.axis_index("tile")
    owned = image.shape[0]
    shots = count // SECTIONS
    pairs = shots * NF
    cap = max(1, CELLS // count)
    pair = me // 2
    shot, freq = pair // NF, pair % NF

    my_ids = me * owned + jnp.arange(owned, dtype=jnp.int32)
    matches = (tile_at[None] == my_ids[:, None, None]).astype(jnp.int32)
    place_row = jnp.arange(tile_at.shape[0], dtype=jnp.int32)[None, :, None]
    place_column = jnp.arange(tile_at.shape[1], dtype=jnp.int32)[None, None, :]
    spot = place_column // SIDE * CELLS + place_row * SIDE + place_column % SIDE
    spots = total_of(matches * spot, (1, 2))
    homes = spots // CELLS
    earlier = (homes[:, None] == homes[None, :]) & (spots[None, :] < spots[:, None])
    ranks = total_of(earlier, 1)
    slot_id = jnp.arange(shots * cap, dtype=jnp.int32)
    wanted = aperture_block[slot_id // cap]
    picks = total_of(
        ((homes[None, :] == wanted[:, None]) & (ranks[None, :] == (slot_id % cap)[:, None])).astype(jnp.int32)
        * jnp.arange(owned, dtype=jnp.int32)[None, :],
        1,
    )

    block = aperture_block[shot]
    window_ids = lax.dynamic_slice(tile_at, (jnp.int32(0), block * SIDE), (SIDE, SIDE)).reshape(CELLS)
    owners = window_ids // owned
    order = jnp.arange(CELLS, dtype=jnp.int32)
    before = (owners[:, None] == owners[None, :]) & (order[None, :] < order[:, None])
    window_slot = owners * cap + total_of(before, 1)
    places = total_of(
        (window_slot[None, :] == jnp.arange(count * cap, dtype=jnp.int32)[:, None]).astype(jnp.int32) * order[None, :], 1
    )

    chosen = freq_index[shot, freq]
    angular = ((chosen + 1).astype(F32) / NFT).reshape(1)
    phase = lax.dynamic_slice(wave_phase, (chosen, jnp.int32(0)), (1, A))
    numbers = jnp.stack([(me % 2 == 0).astype(jnp.int32), source_cell[shot, 0], source_cell[shot, 1]])
    turns = 2.0 * np.pi / A * (np.outer(np.arange(A), np.arange(A)) % A)
    table_cos = jnp.asarray(np.cos(turns), F32)
    table_sin = jnp.asarray(np.sin(turns), F32)

    model = jnp.concatenate([image, slowness], axis=1).reshape(owned, 2 * NZ, 8, 128)
    smem = pl.BlockSpec(memory_space=pltpu.SMEM)
    vmem = pl.BlockSpec(memory_space=pltpu.VMEM)

    got_model, got_rows = pl.pallas_call(
        functools.partial(scatter_kernel, count, cap),
        out_shape=(
            jax.ShapeDtypeStruct((count * cap, 2 * NZ, 8, 128), F32),
            jax.ShapeDtypeStruct((SECTIONS, 2, ROWS, A), F32),
        ),
        in_specs=[smem, vmem, vmem],
        out_specs=(vmem, vmem),
        scratch_shapes=[
            pltpu.VMEM((shots * cap, 2 * NZ, 8, 128), F32),
            pltpu.SemaphoreType.DMA((pairs,)),
            pltpu.SemaphoreType.DMA((count,)),
            pltpu.SemaphoreType.DMA((NF,)),
            pltpu.SemaphoreType.DMA((SECTIONS,)),
            pltpu.SemaphoreType.DMA,
        ],
        compiler_params=pltpu.CompilerParams(collective_id=0, has_side_effects=True, vmem_limit_bytes=VMEM_LIMIT),
    )(picks, model, observed[0])

    tiles = pl.pallas_call(
        march_kernel,
        out_shape=jax.ShapeDtypeStruct((CELLS, NZ, 8, 128), F32),
        in_specs=[smem, smem, smem, vmem, vmem, vmem, vmem, vmem],
        out_specs=vmem,
        scratch_shapes=[
            pltpu.VMEM((NZ, 2, A, 128), F32),
            pltpu.VMEM((NZ, 2, A, 128), F32),
            pltpu.VMEM((NZ, 2, A, A), F32),
            pltpu.VMEM((NZ, 2, A, A), F32),
            pltpu.VMEM((2, A, A), F32),
            pltpu.VMEM((4, 2 * A, 2 * A), BF16),
            pltpu.VMEM((4, 2 * A, 2 * A), BF16),
        ],
        compiler_params=pltpu.CompilerParams(vmem_limit_bytes=VMEM_LIMIT),
    )(numbers, window_slot, angular, phase, table_cos, table_sin, got_model, got_rows)

    out = pl.pallas_call(


        (lambda places, ranks, homes, blocks, *rest: return_kernel(count, cap, places, owned, ranks, homes, blocks, *rest)),
        out_shape=jax.ShapeDtypeStruct((owned, NZ, 8, 128), F32),
        in_specs=[smem, smem, smem, smem, vmem],
        out_specs=vmem,
        scratch_shapes=[
            pltpu.VMEM((pairs, cap, NZ, 8, 128), F32),
            pltpu.VMEM((count, cap, NZ, 8, 128), F32),
            pltpu.SemaphoreType.DMA((count,)),
            pltpu.SemaphoreType.DMA((pairs,)),
            pltpu.SemaphoreType.DMA,
        ],
        compiler_params=pltpu.CompilerParams(collective_id=1, has_side_effects=True, vmem_limit_bytes=VMEM_LIMIT),
    )(places, ranks, homes, aperture_block, tiles)
    return out.reshape(owned, NZ, TL * TL)


def solution(mesh):
    return jax.shard_map(
        shards,
        mesh=mesh,
        in_specs=(
            P(),
            P(),
            P("group"),
            P("group", None),
            P("group", None),
            P(("group", "tile"), None, None, None, None),
            P(("group", "tile"), None, None),
            P(("group", "tile"), None, None),
        ),
        out_specs=P(("group", "tile"), None, None),
        check_vma=False,
    )
```

```python
import functools
import math

import jax
import jax.numpy as jnp
import numpy as np
from jax import lax
from jax.experimental import pallas as pl
from jax.experimental.pallas import tpu as pltpu
from jax.sharding import PartitionSpec as P

A = 256
TL = 32
SIDE = A // TL
CELLS = SIDE * SIDE
SECTIONS = 4
NZ = 4
NF = 2
NFT = 600
ROWS = A // SECTIONS
LENS_GAIN = 3.0
VMEM_LIMIT = 56 * 1024 * 1024

F32 = jnp.float32
BF16 = jnp.bfloat16


def sin_cos(angle):
    t = angle * 0.5
    u = t * t
    s = -1.0 / math.factorial(11)
    for n in (9, 7, 5, 3, 1):
        s = s * u + (-1.0) ** (n // 2) / math.factorial(n)
    s = s * t
    c = 1.0 / math.factorial(12)
    for n in (10, 8, 6, 4, 2, 0):
        c = c * u + (-1.0) ** (n // 2) / math.factorial(n)
    return 2.0 * s * c, 1.0 - 2.0 * s * s


def split(values):
    high = values.astype(BF16)
    return high, (values - high.astype(F32)).astype(BF16)


def dot(a, b):
    return lax.dot_general(a, b, (((1,), (0,)), ((), ())), preferred_element_type=F32)


def swap_groups(tiles):
    lane = lax.broadcasted_iota(jnp.int32, tiles[0].shape, tiles[0].ndim - 1)
    axis = tiles[0].ndim - 1

    def exchange(low, high, width, first):
        return (
            jnp.where(first, low, pltpu.roll(high, width, axis)),
            jnp.where(first, pltpu.roll(low, 128 - width, axis), high),
        )

    first = lane < 64
    a0, a2 = exchange(tiles[0], tiles[2], 64, first)
    a1, a3 = exchange(tiles[1], tiles[3], 64, first)
    first = (lane & 32) == 0
    b0, b1 = exchange(a0, a1, 32, first)
    b2, b3 = exchange(a2, a3, 32, first)
    return b0, b1, b2, b3


def greet_all(me, count):
    barrier = pltpu.get_barrier_semaphore()

    def signal(step, carry):
        pl.semaphore_signal(
            barrier,
            inc=1,
            device_id={"tile": lax.rem(me + step, count)},
            device_id_type=pl.DeviceIdType.MESH,
        )
        return carry

    lax.fori_loop(1, count, signal, 0)
    pl.semaphore_wait(barrier, count - 1)


def remote(src, dst, send_sem, recv_sem, target):
    return pltpu.make_async_remote_copy(
        src_ref=src,
        dst_ref=dst,
        send_sem=send_sem,
        recv_sem=recv_sem,
        device_id={"tile": target},
        device_id_type=pl.DeviceIdType.MESH,
    )


def index_kernel(count, cap, owned, tile_at, blocks, source_cell, freq_index, wave_phase,
                 picks, window_slot, places, homes, ranks, numbers, angular, phase, own_at, seen, rows, sem):
    me = lax.axis_index("tile")
    shots = count // SECTIONS
    shot = jnp.clip(lax.div(me, 2) - shots // 2, 0, shots - 1)
    chosen = freq_index[shot, lax.rem(me, 2)]
    first = lax.div(chosen, 8) * 8
    fetch = pltpu.make_async_copy(wave_phase.at[pl.ds(pl.multiple_of(first, 8), 8)], rows, sem)
    fetch.start()
    windows = tile_at.shape[1] // SIDE

    def clear(ref, size):
        def one(i, carry):
            ref[i] = 0
            return carry

        lax.fori_loop(0, size, one, 0)

    clear(own_at, windows * cap)
    clear(seen, count)
    clear(places, count * cap)

    def spot(window, place):
        return tile_at[lax.div(place, SIDE), window * SIDE + lax.rem(place, SIDE)]

    def in_window(window, carry):
        def look(place, rank):
            mine = spot(window, place) - me * owned
            held = (mine >= 0) & (mine < owned)

            @pl.when(held)
            def _():
                homes[mine] = window
                ranks[mine] = rank
                own_at[window * cap + rank] = mine

            return rank + held.astype(jnp.int32)

        lax.fori_loop(0, CELLS, look, 0)
        return carry

    lax.fori_loop(0, windows, in_window, 0)

    def pick(slot, carry):
        picks[slot] = own_at[blocks[lax.div(slot, cap)] * cap + lax.rem(slot, cap)]
        return carry

    lax.fori_loop(0, shots * cap, pick, 0)
    window = blocks[shot]

    def order(place, carry):
        owner = lax.div(spot(window, place), owned)
        rank = seen[owner]
        seen[owner] = rank + 1
        window_slot[place] = owner * cap + rank
        places[owner * cap + rank] = place
        return carry

    lax.fori_loop(0, CELLS, order, 0)
    numbers[0] = source_cell[shot, 0]
    numbers[1] = source_cell[shot, 1]
    angular[0] = (chosen + 1).astype(F32) / NFT
    fetch.wait()
    phase[...] = rows[pl.ds(lax.rem(chosen, 8), 1)]


def whole(ref, *at):
    return jnp.concatenate([ref[(*at, 0)], ref[(*at, 1)]], axis=1)


def build_operators(phase, table_cos, table_sin, left_ops, right_ops):
    s, c = sin_cos(jnp.broadcast_to(phase[...], (8, A)))

    def table_dot(a, b):
        return lax.dot_general(
            a, b, (((1,), (0,)), ((), ())), preferred_element_type=F32, precision=lax.Precision.HIGHEST
        )

    c_cos, c_sin = table_dot(c, table_cos[...]), table_dot(c, table_sin[...])
    s_cos, s_sin = table_dot(s, table_cos[...]), table_dot(s, table_sin[...])
    scale = 1.0 / A

    def turned(row):
        return pltpu.roll(jnp.broadcast_to(row[0:1], (A, A)), 0, 1, stride=1, stride_axis=0)

    o_re, o_im = turned((c_cos + s_sin) * scale), turned((s_cos - c_sin) * scale)
    t_re, t_im = turned((c_cos - s_sin) * scale), turned((s_cos + c_sin) * scale)

    def put(ref, which, blocks, left):
        for i, block in enumerate(blocks):
            high, low = split(block)
            for third, part in enumerate((high, high, low)):
                a, b = (i // 2) * A, (i % 2) * A
                if left:
                    ref[which, pl.ds(a, A), pl.ds(third * 2 * A + b, A)] = part
                else:
                    ref[which, pl.ds(third * 2 * A + a, A), pl.ds(b, A)] = part

    put(left_ops, 0, (o_re, -o_im, o_im, o_re), True)
    put(left_ops, 1, (t_re, t_im, -t_im, t_re), True)
    put(right_ops, 0, (t_re, t_im, -t_im, t_re), False)
    put(right_ops, 1, (o_re, -o_im, o_im, o_re), False)


def both_sides(left_ops, right_ops, which, re, im):
    high, low = split(jnp.concatenate([re, im], axis=0))
    left = dot(left_ops[which], jnp.concatenate([high, low, high], axis=0))
    high, low = split(jnp.concatenate([left[:A], left[A:]], axis=1))
    right = dot(jnp.concatenate([high, low, high], axis=1), right_ops[which])
    return right[:, :A], right[:, A:]


def gather(got, window_slot, cells):
    def one(block_row, carry):
        for half in range(SIDE // 4):
            slots = [window_slot[block_row * SIDE + half * 4 + j] for j in range(4)]
            for z in range(NZ):
                tiles = [got[slot, pl.ds(z, 8, stride=NZ)] for slot in slots]
                for k, part in enumerate(swap_groups(tiles)):
                    cells[z, half, pl.ds(block_row * TL + k, 8, stride=4)] = part
        return carry

    lax.fori_loop(0, SIDE, one, 0)


def migrate_kernel(
    count, cap, owned,
    picks, window_slot, places, homes, ranks, numbers, angular_ref, blocks,
    phase, table_cos, table_sin, image, slowness, observed,
    out,
    packed, got_slow, got_image, rows, cells, reflect, partial, lens, fields, spare, left_ops, right_ops,
    tiles, half_sums, sibling_sums, sums, got_sums,
    send_sem, recv_sem, forward_sem, row_send, row_recv, swap_send, swap_recv, sum_send, sum_recv,
):
    me = lax.axis_index("tile")
    got = (got_slow, got_image)
    shots = count // SECTIONS
    chip, core = lax.div(me, 2), lax.rem(me, 2)
    shot = chip - shots // 2
    computes = (shot >= 0) & (shot < shots)
    sibling = me + 1 - 2 * core
    section, column = lax.div(me, shots), lax.rem(me, shots)

    def marcher(shot_id, freq):
        return 2 * (shot_id + shots // 2) + freq

    greet_all(me, count)

    def pack(slot, carry):
        tile = picks[slot]
        for kind, source in enumerate((slowness, image)):
            levels = source[tile]
            for chunk in range(8):
                packed[kind, slot, pl.ds(chunk * NZ, NZ)] = levels[:, chunk * 128 : chunk * 128 + 128]
        return carry

    lax.fori_loop(0, shots * cap, pack, 0)

    def model_copy(kind, to):
        return remote(
            packed.at[kind, pl.ds(to * cap, cap)],
            got[kind].at[pl.ds(me * cap, cap)],
            send_sem.at[kind, to],
            recv_sem.at[kind, me],
            marcher(to, core),
        )

    def send_model(kind):
        def send(step, carry):
            to = lax.rem(column + step, shots)

            @pl.when(marcher(to, core) != me)
            def _():
                model_copy(kind, to).start()

            @pl.when(marcher(to, core) == me)
            def _():
                for slot in range(cap):
                    got[kind][me * cap + slot] = packed[kind, to * cap + slot]

            return carry

        lax.fori_loop(0, shots, send, 0)

    def rows_copy(freq):
        return remote(
            observed.at[0, freq], rows.at[section], row_send.at[freq], row_recv.at[section], marcher(column, freq)
        )

    send_model(0)
    send_model(1)
    for freq in range(NF):

        @pl.when(marcher(column, freq) != me)
        def _():
            rows_copy(freq).start()

        @pl.when(marcher(column, freq) == me)
        def _():
            rows[section] = observed[0, freq]

    def forward_copy(kind, step):
        source = lax.rem(me + 2 * step, count)
        block = got[kind].at[pl.ds(source * cap, cap)]
        return remote(block, block, forward_sem.at[kind, step], recv_sem.at[kind, source], sibling)

    def arrival(kind, source):
        return remote(
            packed.at[kind, pl.ds(0, cap)],
            got[kind].at[pl.ds(source * cap, cap)],
            send_sem.at[kind, 0],
            recv_sem.at[kind, source],
            sibling,
        )

    def forward(kind):
        forward_copy(kind, 0).start()

        def one(step, carry):
            arrival(kind, lax.rem(me + 2 * step, count)).wait_recv()
            forward_copy(kind, step).start()
            return carry

        lax.fori_loop(1, count // 2, one, 0)

    def arrive(kind):
        def one(step, carry):
            arrival(kind, lax.rem(sibling + 2 * step, count)).wait_recv()
            return carry

        lax.fori_loop(0, count // 2, one, 0)

    def swap_copy(z):
        return remote(half_sums.at[z, 1 - core], sibling_sums.at[z], swap_send.at[z], swap_recv.at[z], sibling)

    def sum_copy(z, step):
        owner = lax.rem(me + 2 * step, count)
        return remote(
            sums.at[z, lax.div(owner, 2)], got_sums.at[z, shot], sum_send.at[z, step], sum_recv.at[z, shot], owner
        )

    def finish_level(z):
        swap_copy(z).wait_recv()
        sums[z] = half_sums[z, core] + sibling_sums[z]

        def one(step, carry):
            sum_copy(z, step).start()
            return carry

        lax.fori_loop(1, count // 2, one, 0)
        got_sums[z, shot] = sums[z, lax.div(me, 2)]

    @pl.when(computes)
    def _():
        angular = angular_ref[0]
        build_operators(phase, table_cos, table_sin, left_ops, right_ops)
        row_id = lax.broadcasted_iota(jnp.int32, (A, A), 0)
        column_id = lax.broadcasted_iota(jnp.int32, (A, A), 1)
        spare[0] = jnp.where((row_id == numbers[0]) & (column_id == numbers[1]), float(A), 0.0).astype(F32)
        spare[1] = jnp.zeros((A, A), F32)
        forward(0)
        arrive(0)
        gather(got[0], window_slot, cells)

        def extend(z, re, im):
            c, s = lens[z, 0], lens[z, 1]
            return both_sides(left_ops, right_ops, 0, c * re - s * im, c * im + s * re)

        def down(z, carry):
            s, c = sin_cos(whole(cells, z) * (LENS_GAIN * angular))
            lens[z, 0] = c
            lens[z, 1] = s
            re, im = extend(z, spare[0], spare[1])
            spare[0] = re
            spare[1] = im
            fields[z, 0] = re
            fields[z, 1] = im

            @pl.when(z == 2)
            def _():
                forward(1)

            return carry

        lax.fori_loop(0, NZ, down, 0)
        arrive(1)
        gather(got[1], window_slot, reflect)
        spare[...] = jnp.zeros_like(spare)

        def up(step, carry):
            z = NZ - 1 - step
            weight = whole(reflect, z) * angular
            re, im = extend(z, spare[0] - weight * fields[z, 1], spare[1] + weight * fields[z, 0])
            spare[0] = re
            spare[1] = im
            return carry

        lax.fori_loop(0, NZ, up, 0)
        for part in range(SECTIONS):

            @pl.when(part * shots + shot != me)
            def _():
                remote(observed.at[0, 0], rows.at[part], row_send.at[0], row_recv.at[part], sibling).wait_recv()

            for half in range(2):
                at = (half, pl.ds(part * ROWS, ROWS))
                spare[at] = spare[at] - rows[part, half]

        def back(z, carry):
            re, im = both_sides(left_ops, right_ops, 1, spare[0], spare[1])
            c, s = lens[z, 0], lens[z, 1]
            re, im = c * re + s * im, c * im - s * re
            spare[0] = re
            spare[1] = im
            image_part = angular * (im * fields[z, 0] - re * fields[z, 1])
            partial[0] = image_part[:, :128]
            partial[1] = image_part[:, 128:]

            def cut(block_row, carry):
                for half in range(SIDE // 4):
                    parts = [partial[half, pl.ds(block_row * TL + k, 8, stride=4)] for k in range(4)]
                    for j, tile in enumerate(swap_groups(parts)):
                        tiles[block_row * SIDE + half * 4 + j] = tile
                return carry

            lax.fori_loop(0, SIDE, cut, 0)

            def put(spot, carry):
                for parity in range(2):
                    for slot in range(cap):
                        half_sums[z, parity, spot, slot] = tiles[places[(2 * spot + parity) * cap + slot]]
                return carry

            lax.fori_loop(0, count // 2, put, 0)
            swap_copy(z).start()

            @pl.when(z > 0)
            def _():
                finish_level(z - 1)

            return carry

        lax.fori_loop(0, NZ, back, 0)
        finish_level(NZ - 1)

    def sum_arrives(index, carry):
        z, source = lax.div(index, shots), lax.rem(index, shots)

        @pl.when(marcher(source, core) != me)
        def _():
            remote(
                sums.at[0, 0], got_sums.at[z, source], sum_send.at[0, 0], sum_recv.at[z, source], marcher(source, core)
            ).wait_recv()

        return carry

    lax.fori_loop(0, NZ * shots, sum_arrives, 0)

    def collect(tile, carry):
        for z in range(NZ):

            def add(source, total):
                mine = homes[tile] == blocks[source]
                return total + jnp.where(mine, got_sums[z, source, ranks[tile]], 0.0)

            total = lax.fori_loop(0, shots, add, jnp.zeros((8, 128), F32), unroll=shots <= 4)
            for chunk in range(8):
                out[tile, pl.ds(z, 1), pl.ds(chunk * 128, 128)] = total[chunk : chunk + 1]
        return carry

    lax.fori_loop(0, owned, collect, 0)

    def model_left(to, carry):
        @pl.when(marcher(to, core) != me)
        def _():
            model_copy(0, to).wait_send()
            model_copy(1, to).wait_send()

        return carry

    lax.fori_loop(0, shots, model_left, 0)
    for freq in range(NF):

        @pl.when(marcher(column, freq) != me)
        def _():
            rows_copy(freq).wait_send()

    @pl.when(computes)
    def _():
        def forwards_left(step, carry):
            forward_copy(0, step).wait_send()
            forward_copy(1, step).wait_send()
            return carry

        lax.fori_loop(0, count // 2, forwards_left, 0)

        def level_left(z, carry):
            swap_copy(z).wait_send()

            def one(step, carry):
                sum_copy(z, step).wait_send()
                return carry

            return lax.fori_loop(1, count // 2, one, carry)

        lax.fori_loop(0, NZ, level_left, 0)


def shards(wave_phase, tile_at, aperture_block, source_cell, freq_index, observed, image, slowness):
    count = lax.axis_size("tile")
    owned = image.shape[0]
    shots = count // SECTIONS
    cap = max(1, CELLS // count)
    windows = tile_at.shape[1] // SIDE
    smem = pl.BlockSpec(memory_space=pltpu.SMEM)
    vmem = pl.BlockSpec(memory_space=pltpu.VMEM)

    def ints(*shape):
        return jax.ShapeDtypeStruct(shape, jnp.int32)

    *tables, phase = pl.pallas_call(
        functools.partial(index_kernel, count, cap, owned),
        out_shape=(
            ints(shots * cap), ints(CELLS), ints(count * cap), ints(owned), ints(owned), ints(2),
            jax.ShapeDtypeStruct((1,), F32),
            jax.ShapeDtypeStruct((1, A), F32),
        ),
        in_specs=[smem, smem, smem, smem, pl.BlockSpec(memory_space=pl.ANY)],
        out_specs=(smem,) * 7 + (vmem,),
        scratch_shapes=[
            pltpu.SMEM((windows * cap,), jnp.int32),
            pltpu.SMEM((count,), jnp.int32),
            pltpu.VMEM((8, A), F32),
            pltpu.SemaphoreType.DMA,
        ],
    )(tile_at, aperture_block, source_cell, freq_index, wave_phase)

    turns = 2.0 * np.pi / A * (np.outer(np.arange(A), np.arange(A)) % A)
    table_cos = jnp.asarray(np.cos(turns), F32)
    table_sin = jnp.asarray(np.sin(turns), F32)
    dma = pltpu.SemaphoreType.DMA
    return pl.pallas_call(
        functools.partial(migrate_kernel, count, cap, owned),
        out_shape=jax.ShapeDtypeStruct((owned, NZ, TL * TL), F32),
        in_specs=[smem] * 8 + [vmem] * 6,
        out_specs=vmem,
        scratch_shapes=[
            pltpu.VMEM((2, shots * cap, 8 * NZ, 128), F32),
            pltpu.VMEM((count * cap, 8 * NZ, 128), F32),
            pltpu.VMEM((count * cap, 8 * NZ, 128), F32),
            pltpu.VMEM((SECTIONS, 2, ROWS, A), F32),
            pltpu.VMEM((NZ, 2, A, 128), F32),
            pltpu.VMEM((NZ, 2, A, 128), F32),
            pltpu.VMEM((2, A, 128), F32),
            pltpu.VMEM((NZ, 2, A, A), F32),
            pltpu.VMEM((NZ, 2, A, A), F32),
            pltpu.VMEM((2, A, A), F32),
            pltpu.VMEM((2, 2 * A, 6 * A), BF16),
            pltpu.VMEM((2, 6 * A, 2 * A), BF16),
            pltpu.VMEM((CELLS, 8, 128), F32),
            pltpu.VMEM((NZ, 2, count // 2, cap, 8, 128), F32),
            pltpu.VMEM((NZ, count // 2, cap, 8, 128), F32),
            pltpu.VMEM((NZ, count // 2, cap, 8, 128), F32),
            pltpu.VMEM((NZ, shots, cap, 8, 128), F32),
            dma((2, shots)),
            dma((2, count)),
            dma((2, count // 2)),
            dma((NF,)),
            dma((SECTIONS,)),
            dma((NZ,)),
            dma((NZ,)),
            dma((NZ, count // 2)),
            dma((NZ, shots)),
        ],
        compiler_params=pltpu.CompilerParams(collective_id=0, has_side_effects=True, vmem_limit_bytes=VMEM_LIMIT),
    )(*tables, aperture_block, phase, table_cos, table_sin, image, slowness, observed)


def solution(mesh):
    return jax.shard_map(
        shards,
        mesh=mesh,
        in_specs=(
            P(),
            P(),
            P("group"),
            P("group", None),
            P("group", None),
            P(("group", "tile"), None, None, None, None),
            P(("group", "tile"), None, None),
            P(("group", "tile"), None, None),
        ),
        out_specs=P(("group", "tile"), None, None),
        check_vma=False,
    )
```
